32 devices in a mesh: tm: 16 (over z, y, x), tensor: 2 (over core).
Axes of the slice: x: 2, y: 2, z: 4, core: 2. Of those that a mesh axis runs over, the one named last changes fastest.
Arguments:
- query_input: bfloat16 [6144, 2048], P('tm', 'tensor'), may hold values from -6 to 6
- key_input: bfloat16 [6144, 2048], P('tm', 'tensor'), may hold values from -6 to 6
- value_input: bfloat16 [6144, 2048], P('tm', 'tensor'), may hold values from -6 to 6
- log_decay: float32 [16, 6144], P('tensor', 'tm'), may hold values from -0.75 to 0, as said below
- stretch_ids: int32 [6144], P('tm'), may hold values from 0 to 95, as said below
- norm_gain: float32 [2048], P('tensor'), may hold values from 0.1 to 1.9
- out_weight: bfloat16 [2048, 4096], P('tensor'), may hold values from -0.125 to 0.125
- out_cotangent: bfloat16 [6144, 4096], P(('tm', 'tensor')), may hold values from -6 to 6
Outputs:
- layer_out: bfloat16 [6144, 4096], P(('tm', 'tensor'))
- query_grad: bfloat16 [6144, 2048], P('tm', 'tensor')
- key_grad: bfloat16 [6144, 2048], P('tm', 'tensor')
- value_grad: bfloat16 [6144, 2048], P('tm', 'tensor')
The draws below stay inside these ranges and needn't reach their ends.
Inputs may be any that keep to these rules, and one draw needn't show every extreme that they name: `stretch_ids`: stretch ids never fall along the tokens, start at 0 and rise by at most one at a time, change only at multiples of 32 tokens, and rise at every multiple of 384 tokens, so that no stretch crosses a block; every block holds exactly 6 stretches. `log_decay`: every entry is negative.
All inputs are finite; a program needn't handle non-finite values.
Results may differ from the reference program's by a relative error of at most 0.014.
Values may be sent and summed in bfloat16 or wider, within the bound.
A program may use at most 64 MiB of HBM per device.

```python
import math
import jax
import jax.numpy as jnp
from jax import lax

LOCAL_HEADS = 16
HD = 128
DOUT = 4096
FRAME = 32
TOK_DEV = 384
SEQUENCE_TOKENS = 6144
N_TM = 16
N_TENSOR = 2


def draw_log_decay(key, part):
    random_key_list = jax.random.split(jax.random.fold_in(key, 11), 6)
    fast_share = 0.5
    fast_head = jax.random.uniform(random_key_list[0], (LOCAL_HEADS, 1)) < fast_share
    fast_span = jnp.exp(jax.random.uniform(random_key_list[1], (LOCAL_HEADS, 1), minval=math.log(30.0), maxval=math.log(50.0)))
    slow_total = jnp.exp(jax.random.uniform(random_key_list[2], (LOCAL_HEADS, 1), minval=math.log(0.1), maxval=math.log(0.8)))
    baseline_decay_rate = jnp.where(fast_head, 1.0 / fast_span, slow_total / SEQUENCE_TOKENS)
    jagged_level = jax.random.uniform(random_key_list[3], (LOCAL_HEADS, SEQUENCE_TOKENS), minval=0.5, maxval=1.5)
    spike_positions = jax.random.randint(random_key_list[4], (LOCAL_HEADS, 2), 0, SEQUENCE_TOKENS)
    loss_values = jax.random.uniform(random_key_list[5], (LOCAL_HEADS, 2), minval=0.22, maxval=0.69)
    position_list = jnp.arange(SEQUENCE_TOKENS)[None, :]
    spike_events = jnp.where(position_list == spike_positions[:, 0:1], loss_values[:, 0:1], 0.0) + jnp.where(position_list == spike_positions[:, 1:2], loss_values[:, 1:2], 0.0)
    return (-(baseline_decay_rate * jagged_level + spike_events)).astype(jnp.float32)


def draw_stretch_ids(key, part):
    block_count = SEQUENCE_TOKENS // TOK_DEV
    frames_block = TOK_DEV // FRAME
    starts_block = max(1, frames_block // 2)
    block_keys = jax.random.split(jax.random.fold_in(key, 23), block_count)

    def block_starts(block_key):
        ranking = jax.random.permutation(block_key, jnp.arange(max(frames_block - 1, 1), dtype=jnp.int32))
        rest = (ranking[:frames_block - 1] < starts_block - 1).astype(jnp.int32)
        return jnp.concatenate([jnp.ones((1,), jnp.int32), rest])
    new_stretch = jax.vmap(block_starts)(block_keys).reshape(block_count * frames_block)
    stretch_index = jnp.cumsum(new_stretch) - 1
    return jnp.repeat(stretch_index, FRAME, total_repeat_length=SEQUENCE_TOKENS).astype(jnp.int32)


def block_scale(key, extent, cuts, low, top_value):
    def one(axis_at, shards_of):
        heights = jax.random.uniform(jax.random.fold_in(jax.random.fold_in(key, 6), axis_at), (shards_of,), jnp.float32, low / len(cuts), top_value / len(cuts))
        return jnp.repeat(jnp.exp(heights), extent[axis_at] // shards_of).reshape((-1,) + (1,) * (len(extent) - axis_at - 1))

    loudness = one(*cuts[0])
    for cut in cuts[1:]:
        loudness = loudness * one(*cut)
    return loudness


def gaussian(key, extent, deviation, limit, pieces=(), kind=jnp.bfloat16):
    gain = block_scale(key, extent, pieces, -0.22, 0.18) if pieces else 1.0
    array = jax.random.normal(key, extent, jnp.float32) * deviation * gain
    return jnp.minimum(jnp.maximum(array, -limit), limit).astype(kind)


def setup_inputs(seed: int = 0) -> dict:
    key_of = jax.random.split(jax.random.key(seed), 9)
    return {
        "query_input": gaussian(key_of[0], (SEQUENCE_TOKENS, LOCAL_HEADS * HD), 1.0, 6.0, ((0, 16), (1, 2))),
        "key_input": gaussian(key_of[1], (SEQUENCE_TOKENS, LOCAL_HEADS * HD), 1.0, 6.0, ((0, 16), (1, 2))),
        "value_input": gaussian(key_of[2], (SEQUENCE_TOKENS, LOCAL_HEADS * HD), 1.0, 6.0, ((0, 16), (1, 2))),
        "log_decay": draw_log_decay(jax.random.fold_in(key_of[8], 71), 0),
        "stretch_ids": draw_stretch_ids(jax.random.fold_in(key_of[8], 71), 0),
        "norm_gain": jnp.clip(1.0 + 0.18 * jax.random.normal(key_of[5], (LOCAL_HEADS * HD,), jnp.float32), 0.1, 1.9),
        "out_weight": gaussian(key_of[6], (LOCAL_HEADS * HD, DOUT), (LOCAL_HEADS * HD) ** -0.5, 0.125, ((0, 2),)),
        "out_cotangent": gaussian(key_of[7], (SEQUENCE_TOKENS, DOUT), 1.0, 6.0, ((0, 32),)),
    }


def local_parts(query_blk, key_blk, decay_blk, stretch_blk):
    query_pos = jnp.maximum(query_blk, 0)
    key_pos = jnp.maximum(key_blk, 0)
    cumulative = jnp.cumsum(decay_blk, axis=1)
    same_stretch = stretch_blk[:, None] == stretch_blk[None, :]
    visible = stretch_blk[None, :] <= stretch_blk[:, None]
    stretch_end = lax.optimization_barrier(jnp.min(jnp.where(same_stretch[None], cumulative[:, None, :], jnp.inf), axis=2))
    block_end = cumulative[:, -1]
    weights = jnp.where(visible[None], jnp.exp(jnp.minimum(stretch_end[:, :, None] - cumulative[:, None, :], 0.0)), 0.0)
    scores = jnp.einsum('iha,jha->hij', query_pos.astype(jnp.float32), key_pos.astype(jnp.float32))
    probs = lax.optimization_barrier((weights * scores).astype(jnp.bfloat16)).astype(jnp.float32)
    key_scale = jnp.exp(block_end[:, None] - cumulative).T
    decayed = lax.optimization_barrier((key_scale[:, :, None] * key_pos).astype(jnp.bfloat16)).astype(jnp.float32)
    end_scale = jnp.exp(stretch_end).T
    return (query_pos, key_pos, weights, probs, key_scale, decayed, end_scale, jnp.exp(block_end))

def reference(query_input, key_input, value_input, log_decay, stretch_ids, norm_gain, out_weight, out_cotangent):
    highest = lax.Precision.HIGHEST
    blocks = N_TM
    shape_four = (blocks, TOK_DEV, LOCAL_HEADS, HD)
    query_blocks = query_input.reshape(shape_four)
    key_blocks = key_input.reshape(shape_four)
    value_blocks = value_input.reshape(shape_four)
    decay_blocks = log_decay.reshape(LOCAL_HEADS, blocks, TOK_DEV).transpose(1, 0, 2)
    stretch_blocks = stretch_ids.reshape(blocks, TOK_DEV)

    def forward_step(prefix, inputs):
        query_blk, key_blk, value_blk, decay_blk, stretch_blk = inputs
        query_pos, key_pos, weights, probs, key_scale, decayed, end_scale, block_decay = local_parts(query_blk, key_blk, decay_blk, stretch_blk)
        value_wide = value_blk.astype(jnp.float32)
        local_out = jnp.einsum('hij,jhb->ihb', probs, value_wide)
        carried = jnp.einsum('iha,hab->ihb', query_pos.astype(jnp.float32), prefix, precision=highest)
        mixed = local_out + end_scale[:, :, None] * carried
        state = jnp.einsum('jha,jhb->hab', decayed, value_wide)
        return (block_decay[:, None, None] * prefix + state, (mixed, prefix))
    start_state = jnp.zeros((LOCAL_HEADS, HD, HD), jnp.float32)
    unused_state, (mixed_all, prefix_all) = lax.scan(forward_step, start_state, (query_blocks, key_blocks, value_blocks, decay_blocks, stretch_blocks))
    inv_rms = lax.rsqrt(lax.optimization_barrier(jnp.mean(mixed_all * mixed_all, axis=3)) + 1e-06)
    gain_heads = norm_gain.reshape(LOCAL_HEADS, HD)
    attended = (mixed_all * inv_rms[..., None] * gain_heads).astype(jnp.bfloat16).reshape(SEQUENCE_TOKENS, LOCAL_HEADS * HD)
    group_rows = LOCAL_HEADS // N_TENSOR * HD
    total = jnp.zeros((SEQUENCE_TOKENS, DOUT), jnp.float32)
    for member in range(N_TENSOR):
        partial_out = jnp.dot(attended[:, member * group_rows:(member + 1) * group_rows], out_weight[member * group_rows:(member + 1) * group_rows], preferred_element_type=jnp.float32).astype(jnp.bfloat16)
        total = total + lax.optimization_barrier(partial_out).astype(jnp.float32)
    layer_out = total.astype(jnp.bfloat16)
    out_grad = jnp.dot(out_cotangent, out_weight.T, preferred_element_type=jnp.float32).reshape(shape_four)
    gained = out_grad * gain_heads
    along = lax.optimization_barrier(jnp.mean(mixed_all * gained, axis=3))
    cube = inv_rms * inv_rms * inv_rms
    mixed_grad = (inv_rms[..., None] * gained - mixed_all * (cube * along)[..., None]).astype(jnp.bfloat16)

    def backward_step(later, inputs):
        query_blk, key_blk, value_blk, decay_blk, stretch_blk, grad_blk, prefix = inputs
        query_pos, key_pos, weights, probs, key_scale, decayed, end_scale, block_decay = local_parts(query_blk, key_blk, decay_blk, stretch_blk)
        value_wide = value_blk.astype(jnp.float32)
        grad_wide = lax.optimization_barrier(grad_blk).astype(jnp.float32)
        prob_grad = jnp.einsum('ihb,jhb->hij', grad_wide, value_wide)
        score_grad = lax.optimization_barrier((weights * prob_grad).astype(jnp.bfloat16)).astype(jnp.float32)
        value_local = jnp.einsum('hij,ihb->jhb', probs, grad_wide)
        query_local = jnp.einsum('hij,jha->iha', score_grad, key_pos.astype(jnp.float32))
        key_local = jnp.einsum('hij,iha->jha', score_grad, query_pos.astype(jnp.float32))
        scaled_query = lax.optimization_barrier((end_scale[:, :, None] * query_pos).astype(jnp.bfloat16)).astype(jnp.float32)
        state_grad = jnp.einsum('iha,ihb->hab', scaled_query, grad_wide)
        value_carry = jnp.einsum('jha,hab->jhb', decayed, later, precision=highest)
        key_carry = key_scale[:, :, None] * jnp.einsum('jhb,hab->jha', value_wide, later, precision=highest)
        query_carry = end_scale[:, :, None] * jnp.einsum('ihb,hab->iha', grad_wide, prefix, precision=highest)
        query_grad = jnp.where(query_blk > 0, query_local + query_carry, 0.0).astype(jnp.bfloat16)
        key_grad = jnp.where(key_blk > 0, key_local + key_carry, 0.0).astype(jnp.bfloat16)
        value_grad = (value_local + value_carry).astype(jnp.bfloat16)
        return (state_grad + block_decay[:, None, None] * later, (query_grad, key_grad, value_grad))
    unused_grad, (query_grad, key_grad, value_grad) = lax.scan(backward_step, start_state, (query_blocks, key_blocks, value_blocks, decay_blocks, stretch_blocks, mixed_grad, prefix_all), reverse=True)
    flat = (SEQUENCE_TOKENS, LOCAL_HEADS * HD)
    return (layer_out, query_grad.reshape(flat), key_grad.reshape(flat), value_grad.reshape(flat))
```

```python
import functools

import jax
import jax.numpy as jnp
from jax import lax
from jax.experimental import pallas as pl
from jax.experimental.pallas import tpu as pltpu
from jax.sharding import PartitionSpec as P

EPSILON = 1e-06
F32 = jnp.float32
BF16 = jnp.bfloat16
MESH = pl.DeviceIdType.MESH
NT = (((1,), (1,)), ((), ()))
TN = (((0,), (0,)), ((), ()))
NN = (((1,), (0,)), ((), ()))


def mm(a, b, dims, precision=None):
    return lax.dot_general(a, b, dims, precision=precision, preferred_element_type=F32)


def owners_of(rows, head_size, count):
    owners = count
    while rows % owners or (rows // owners) % 16 or head_size % (rows // owners):
        owners -= 1
    return owners


def kernel(
    n, nt, owners,
    q_ref, k_ref, v_ref, ld_ref, sid_ref, gain_ref, w_hbm, cot_hbm,
    out_ref, qg_ref, kg_ref, vg_ref,
    w, cot, bound, cumrow, kscale, escale, decayed, weights, probs, local, outgrad,
    attended, mixgrad, vlocal, klocal, decays,
    send_s, recv_s, send_p, prefix, send_g, recv_g, send_l, later, send_o, recv_o,
    w_sem, cot_sem, c_send, c_recv, s_send, s_recv, p_send, p_recv,
    g_send, g_recv, l_send, l_recv, o_send, o_recv,
):
    me = lax.axis_index("tm")
    my_t = lax.axis_index("tensor")
    tok = q_ref.shape[0]
    heads = ld_ref.shape[0]
    hd = q_ref.shape[1] // heads
    rows_t = tok // nt
    piece = heads * hd // owners
    per_head = owners // heads
    wide = w.shape[1]

    def other(k):
        return lax.rem(me + k, n)

    def source(k):
        return lax.rem(me + n - k, n)

    def owner_only(index, body):
        if owners == n:
            body()
        else:
            pl.when(index < owners)(body)

    def partners(body, lowest=1, count=n):
        def step(k, carry):
            body(k)
            return carry

        lax.fori_loop(lowest, count, step, 0)

    def each_head(body):
        def step(h, carry):
            body(h, pl.ds(pl.multiple_of(h * hd, hd), hd))
            return carry

        lax.fori_loop(0, heads, step, 0)

    barrier = pltpu.get_barrier_semaphore()
    partners(lambda k: pl.semaphore_signal(
        barrier, inc=1, device_id={"tm": other(k)}, device_id_type=MESH))
    partners(lambda k: pl.semaphore_signal(
        barrier, inc=1, device_id={"tensor": lax.rem(my_t + k, nt)}, device_id_type=MESH), 1, nt)

    w_copy = pltpu.make_async_copy(w_hbm, w, w_sem)
    w_copy.start()
    my_rows = pl.ds(pl.multiple_of(my_t * rows_t, 16), rows_t)
    cot_copy = pltpu.make_async_copy(cot_hbm, cot.at[my_rows], cot_sem)
    cot_copy.start()

    row_id = lax.broadcasted_iota(jnp.int32, (tok, tok), 0)
    col_id = lax.broadcasted_iota(jnp.int32, (tok, tok), 1)
    sid = sid_ref[...].astype(F32)
    sid_row = jnp.broadcast_to(sid, (tok, tok))
    sid_col = jnp.sum(jnp.where(row_id == col_id, sid_row, 0.0), axis=1, keepdims=True)
    visible = sid_row <= sid_col
    bound[...] = jnp.where(visible, 0.0, -1e30)
    ld = ld_ref[...]
    highest = lax.Precision.HIGHEST
    tri = jnp.where(col_id <= row_id, 1.0, 0.0)
    cumrow[...] = mm(ld, tri, NT, highest)
    cumcol = mm(tri, ld, NT, highest)
    cendcol = mm(jnp.where(visible, 1.0, 0.0), ld, NT, highest)
    top = lax.broadcasted_iota(jnp.int32, (16, hd), 0) < 8
    for h in range(heads):
        cum_h = cumcol[:, h : h + 1]
        end_h = cum_h[tok - 1 : tok]
        kscale[h] = jnp.broadcast_to(jnp.exp(end_h - cum_h), (tok, hd))
        escale[h] = jnp.broadcast_to(cendcol[:, h : h + 1], (tok, hd))
        g = jnp.broadcast_to(jnp.exp(end_h), (16, hd))
        high = g.astype(BF16).astype(F32)
        extra = jnp.where(top, high, g - high).astype(BF16)
        for r in range(per_head):
            send_s[h * per_head + r, piece:, :] = extra

    def state_step(h, cols):
        kp = jnp.maximum(k_ref[:, cols], 0).astype(F32)
        dec = (kscale[h] * kp).astype(BF16)
        decayed[:, cols] = dec
        state = mm(dec, v_ref[:, cols], TN).astype(BF16)
        for r in range(per_head):
            send_s[h * per_head + r, :piece, :] = state[r * piece : (r + 1) * piece]

    each_head(state_step)
    pl.semaphore_wait(barrier, n - 1 + nt - 1)

    def to_owner(src, dst, ss, rs, k):
        d = other(k)
        return pltpu.make_async_remote_copy(
            src.at[d if owners == n else jnp.minimum(d, owners - 1)], dst.at[me],
            ss.at[k], rs.at[k], device_id={"tm": d}, device_id_type=MESH)

    def from_any(src, dst, ss, rs, k):
        return pltpu.make_async_remote_copy(
            src.at[0], dst.at[source(k)], ss.at[k], rs.at[k],
            device_id={"tm": other(k)}, device_id_type=MESH)

    slot_me = me if owners == n else jnp.minimum(me, owners - 1)

    def to_any(src, dst, ss, rs, k):
        d = other(k)
        return pltpu.make_async_remote_copy(
            src.at[d], dst.at[slot_me], ss.at[k], rs.at[k],
            device_id={"tm": d}, device_id_type=MESH)

    def from_owner(src, dst, ss, rs, k):
        s = source(k)
        return pltpu.make_async_remote_copy(
            src.at[0], dst.at[s if owners == n else jnp.minimum(s, owners - 1)],
            ss.at[k], rs.at[k], device_id={"tm": other(k)}, device_id_type=MESH)

    def gather_start(src, dst, ss, rs):
        partners(lambda k: owner_only(other(k), lambda: to_owner(src, dst, ss, rs, k).start()))

        def keep():
            dst[me] = src[slot_me]

        owner_only(me, keep)

    def gather_wait(src, dst, ss, rs):
        owner_only(me, lambda: partners(lambda k: from_any(src, dst, ss, rs, k).wait_recv()))

    def spread_start(src, dst, ss, rs):
        def go():
            partners(lambda k: to_any(src, dst, ss, rs, k).start())
            dst[slot_me] = src[me]

        owner_only(me, go)

    def spread_wait(src, dst, ss, rs):
        partners(lambda k: owner_only(
            source(k), lambda: from_owner(src, dst, ss, rs, k).wait_recv()))

    def sends_wait(src_g, dst_g, ss_g, rs_g, src_s, dst_s, ss_s, rs_s):
        partners(lambda k: owner_only(
            other(k), lambda: to_owner(src_g, dst_g, ss_g, rs_g, k).wait_send()))
        owner_only(me, lambda: partners(
            lambda k: to_any(src_s, dst_s, ss_s, rs_s, k).wait_send()))

    fwd_g = (send_s, recv_s, s_send, s_recv)
    fwd_s = (send_p, prefix, p_send, p_recv)
    bwd_g = (send_g, recv_g, g_send, g_recv)
    bwd_s = (send_l, later, l_send, l_recv)

    gather_start(*fwd_g)

    def cot_remote(k):
        return pltpu.make_async_remote_copy(
            cot_hbm, cot.at[my_rows], c_send.at[k], c_recv.at[k],
            device_id={"tensor": lax.rem(my_t + k, nt)}, device_id_type=MESH)

    def cot_arrival(k):
        s = lax.rem(my_t + nt - k, nt)
        return pltpu.make_async_remote_copy(
            cot_hbm, cot.at[pl.ds(pl.multiple_of(s * rows_t, 16), rows_t)],
            c_send.at[k], c_recv.at[k],
            device_id={"tensor": lax.rem(my_t + k, nt)}, device_id_type=MESH)

    partners(lambda k: cot_remote(k).start(), 1, nt)

    def inner_step(h, cols):
        qp = jnp.maximum(q_ref[:, cols], 0)
        kp = jnp.maximum(k_ref[:, cols], 0)
        end = jnp.concatenate([escale[h]] * (tok // hd), axis=1)
        weight = jnp.exp(jnp.minimum(end - cumrow[pl.ds(h, 1), :], bound[...]))
        weights[h] = weight
        p = (weight * mm(qp, kp, NT)).astype(BF16)
        probs[h] = p
        local[:, cols] = mm(p, v_ref[:, cols], NN)
        escale[h] = jnp.exp(escale[h])

    each_head(inner_step)

    gather_wait(*fwd_g)

    def scan_forward():
        def step(b, state):
            send_p[b] = state.astype(BF16)
            got = recv_s[b].astype(F32)
            g = got[piece : piece + 1] + got[piece + 8 : piece + 9]
            decays[pl.ds(b, 1), :] = g
            return g * state + got[:piece]

        lax.fori_loop(0, n, step, jnp.zeros((piece, hd), F32))

    owner_only(me, scan_forward)
    spread_start(*fwd_s)

    w_copy.wait()
    cot_copy.wait()
    partners(lambda k: cot_arrival(k).wait_recv(), 1, nt)
    chunk = 2 * hd if heads % 2 == 0 else hd

    def outgrad_step(c, carry):
        part = pl.ds(pl.multiple_of(c * chunk, chunk), chunk)
        outgrad[:, part] = mm(cot[...], w[part, :], NT)
        return carry

    lax.fori_loop(0, heads * hd // chunk, outgrad_step, 0)

    spread_wait(*fwd_s)

    def head_rows(buffer, h):
        parts = [buffer[h * per_head + r] for r in range(per_head)]
        return parts[0] if per_head == 1 else jnp.concatenate(parts, axis=0)

    def norm_step(h, cols):
        qp = jnp.maximum(q_ref[:, cols], 0)
        es = escale[h]
        mixed = local[:, cols] + es * mm(qp, head_rows(prefix, h), NN)
        inv = lax.rsqrt(jnp.mean(mixed * mixed, axis=1, keepdims=True) + EPSILON)
        gain = gain_ref[:, cols]
        attended[:, cols] = (mixed * inv * gain).astype(BF16)
        gained = outgrad[:, cols] * gain
        along = jnp.mean(mixed * gained, axis=1, keepdims=True)
        mg = (inv * gained - mixed * (inv * inv * inv * along)).astype(BF16)
        mixgrad[:, cols] = mg
        sq = (es * qp.astype(F32)).astype(BF16)
        grad = mm(sq, mg, TN).astype(BF16)
        for r in range(per_head):
            send_g[h * per_head + r] = grad[r * piece : (r + 1) * piece]

    each_head(norm_step)
    gather_start(*bwd_g)

    step_cols = 512

    def project(t, sink):
        rows = pl.ds(pl.multiple_of(t * rows_t, 16), rows_t)

        def step(c, carry):
            part = pl.ds(pl.multiple_of(c * step_cols, step_cols), step_cols)
            sink(part, mm(attended[rows, :], w[:, part], NN))
            return carry

        lax.fori_loop(0, wide // step_cols, step, 0)

    def out_copy(k):
        return pltpu.make_async_remote_copy(
            send_o.at[k - 1], recv_o.at[k - 1], o_send.at[k], o_recv.at[k],
            device_id={"tensor": lax.rem(my_t + k, nt)}, device_id_type=MESH)

    for k in range(1, nt):
        def keep_out(part, value, k=k):
            send_o[k - 1, :, part] = value.astype(BF16)

        project(lax.rem(my_t + k, nt), keep_out)
        out_copy(k).start()

    gather_wait(*bwd_g)

    def scan_backward():
        def step(i, state):
            b = n - 1 - i
            send_l[b] = state.astype(BF16)
            return decays[pl.ds(b, 1), :] * state + recv_g[b].astype(F32)

        lax.fori_loop(0, n, step, jnp.zeros((piece, hd), F32))

    owner_only(me, scan_backward)
    spread_start(*bwd_s)

    def grad_step(h, cols):
        qp = jnp.maximum(q_ref[:, cols], 0)
        kp = jnp.maximum(k_ref[:, cols], 0)
        mg = mixgrad[:, cols]
        sg = (weights[h] * mm(mg, v_ref[:, cols], NT)).astype(BF16)
        vlocal[:, cols] = mm(probs[h], mg, TN)
        klocal[:, cols] = mm(sg, qp, TN)
        qg = mm(sg, kp, NN) + escale[h] * mm(mg, head_rows(prefix, h), NT)
        qg_ref[:, cols] = jnp.where(qp.astype(F32) > 0, qg, 0.0).astype(BF16)

    each_head(grad_step)

    for k in range(1, nt):
        out_copy(k).wait_recv()

    def keep_own(part, value):
        total = value.astype(BF16).astype(F32)
        for k in range(1, nt):
            total += recv_o[k - 1, :, part].astype(F32)
        out_ref[:, part] = total.astype(BF16)

    project(my_t, keep_own)

    spread_wait(*bwd_s)

    def last_step(h, cols):
        lat = head_rows(later, h)
        vg_ref[:, cols] = (vlocal[:, cols] + mm(decayed[:, cols], lat, NN)).astype(BF16)
        kg = klocal[:, cols] + kscale[h] * mm(v_ref[:, cols], lat, NT)
        kg_ref[:, cols] = jnp.where(k_ref[:, cols].astype(F32) > 0, kg, 0.0).astype(BF16)

    each_head(last_step)

    partners(lambda k: cot_remote(k).wait_send(), 1, nt)
    for k in range(1, nt):
        out_copy(k).wait_send()
    sends_wait(*fwd_g, *fwd_s)
    sends_wait(*bwd_g, *bwd_s)


def on_device(n, nt, q, k, v, ld, sid, gain, w, cot):
    tok, width = q.shape
    heads = ld.shape[0]
    hd = width // heads
    wide = w.shape[1]
    rows_t = cot.shape[0]
    owners = owners_of(width, hd, n)
    piece = width // owners
    vmem = pl.BlockSpec(memory_space=pltpu.VMEM)
    hbm = pl.BlockSpec(memory_space=pl.ANY)
    dma = pltpu.SemaphoreType.DMA
    flat16 = pltpu.VMEM((tok, width), BF16)
    flat32 = pltpu.VMEM((tok, width), F32)
    cost = pl.CostEstimate(
        flops=4 * tok * width * wide + 14 * tok * tok * width + 12 * tok * width * hd,
        bytes_accessed=2 * width * wide + 16 * tok * width,
        transcendentals=heads * tok * tok,
    )
    return pl.pallas_call(
        functools.partial(kernel, n, nt, owners),
        out_shape=(
            jax.ShapeDtypeStruct((rows_t, wide), BF16),
            jax.ShapeDtypeStruct((tok, width), BF16),
            jax.ShapeDtypeStruct((tok, width), BF16),
            jax.ShapeDtypeStruct((tok, width), BF16),
        ),
        in_specs=[vmem] * 6 + [hbm] * 2,
        out_specs=(vmem,) * 4,
        scratch_shapes=[
            pltpu.VMEM(w.shape, BF16),
            pltpu.VMEM((tok, wide), BF16),
            pltpu.VMEM((tok, tok), F32),
            pltpu.VMEM((heads, tok), F32),
            pltpu.VMEM((heads, tok, hd), F32),
            pltpu.VMEM((heads, tok, hd), F32),
            flat16,
            pltpu.VMEM((heads, tok, tok), F32),
            pltpu.VMEM((heads, tok, tok), BF16),
            flat32, flat32, flat16, flat16, flat32, flat32,
            pltpu.VMEM((n, hd), F32),
            pltpu.VMEM((owners, piece + 16, hd), BF16),
            pltpu.VMEM((n, piece + 16, hd), BF16),
            pltpu.VMEM((n, piece, hd), BF16),
            pltpu.VMEM((owners, piece, hd), BF16),
            pltpu.VMEM((owners, piece, hd), BF16),
            pltpu.VMEM((n, piece, hd), BF16),
            pltpu.VMEM((n, piece, hd), BF16),
            pltpu.VMEM((owners, piece, hd), BF16),
            pltpu.VMEM((max(nt - 1, 1), rows_t, wide), BF16),
            pltpu.VMEM((max(nt - 1, 1), rows_t, wide), BF16),
            dma, dma, dma((nt,)), dma((nt,)),
            dma((n,)), dma((n,)), dma((n,)), dma((n,)),
            dma((n,)), dma((n,)), dma((n,)), dma((n,)),
            dma((nt,)), dma((nt,)),
        ],
        compiler_params=pltpu.CompilerParams(
            collective_id=0, has_side_effects=True, vmem_limit_bytes=58 * 1024 * 1024
        ),
        cost_estimate=cost,
    )(q, k, v, ld, sid.reshape(1, -1), gain.reshape(1, -1), w, cot)


def solution(mesh):
    n, nt = mesh.shape["tm"], mesh.shape["tensor"]
    return jax.shard_map(
        functools.partial(on_device, n, nt),
        mesh=mesh,
        in_specs=(
            P("tm", "tensor"),
            P("tm", "tensor"),
            P("tm", "tensor"),
            P("tensor", "tm"),
            P("tm"),
            P("tensor"),
            P("tensor", None),
            P(("tm", "tensor"), None),
        ),
        out_specs=(
            P(("tm", "tensor"), None),
            P("tm", "tensor"),
            P("tm", "tensor"),
            P("tm", "tensor"),
        ),
        check_vma=False,
    )
```

```python
import functools

import jax
import jax.numpy as jnp
from jax import lax
from jax.experimental import pallas as pl
from jax.experimental.pallas import tpu as pltpu
from jax.sharding import PartitionSpec as P

EPSILON = 1e-06
F32 = jnp.float32
BF16 = jnp.bfloat16
MESH = pl.DeviceIdType.MESH
NT = (((1,), (1,)), ((), ()))
TN = (((0,), (0,)), ((), ()))
NN = (((1,), (0,)), ((), ()))


def mm(a, b, dims, precision=None):
    return lax.dot_general(a, b, dims, precision=precision, preferred_element_type=F32)


def owners_of(rows, head_size, count):
    owners = count
    while rows % owners or (rows // owners) % 16 or head_size % (rows // owners):
        owners -= 1
    return owners


def kernel(
    n, nt, owners,
    ld_ref, sid_ref, gain_ref, q_hbm, k_hbm, v_hbm, w_hbm, cot_hbm,
    out_ref, qg_ref, kg_ref, vg_ref,
    q_ref, k_ref, v_ref, w, cot, bound, cumrow, kscale, ends, escale, decayed, weights, probs,
    local, outgrad, attended, mixgrad, vlocal, klocal, decays,
    send_s, recv_s, send_p, prefix, send_g, recv_g, send_l, later,
    send_t, recv_t, send_u, recv_u, part_o, recv_o,
    w_sem, cot_sem, q_sem, k_sem, v_sem, c_send, c_recv, s_send, s_recv, p_send, p_recv,
    g_send, g_recv, l_send, l_recv, o_send, o_recv, t_send, t_recv, u_send, u_recv,
):
    group = n // 2
    me = lax.axis_index("tm")
    my_t = lax.axis_index("tensor")
    upper = me >= group
    base = (me // group) * group
    place = me - base
    peer = lax.rem(me + group, n)
    tok = q_ref.shape[0]
    heads = ld_ref.shape[0]
    hd = q_ref.shape[1] // heads
    rows_t = tok // nt
    piece = heads * hd // owners
    per_head = owners // heads
    wide = w.shape[1]

    def other(k):
        return lax.rem(place + k, group)

    def source(k):
        return lax.rem(place + group - k, group)

    def owner_only(index, body):
        if owners == group:
            body()
        else:
            pl.when(index < owners)(body)

    def slot(index):
        return index if owners == group else jnp.minimum(index, owners - 1)

    def partners(body, lowest=1, count=group):
        def step(k, carry):
            body(k)
            return carry

        lax.fori_loop(lowest, count, step, 0)

    def some_heads(body, low, high):
        width = 2 if (high - low) % 2 == 0 else 1

        def step(i, carry):
            for u in range(width):
                h = low + i * width + u
                body(h, pl.ds(pl.multiple_of(h * hd, hd), hd))
            return carry

        lax.fori_loop(0, (high - low) // width, step, 0)

    barrier = pltpu.get_barrier_semaphore()
    partners(lambda k: pl.semaphore_signal(
        barrier, inc=1, device_id={"tm": base + other(k)}, device_id_type=MESH))
    pl.semaphore_signal(barrier, inc=1, device_id={"tm": peer}, device_id_type=MESH)
    partners(lambda k: pl.semaphore_signal(
        barrier, inc=1, device_id={"tensor": lax.rem(my_t + k, nt)}, device_id_type=MESH), 1, nt)

    k_copy = pltpu.make_async_copy(k_hbm, k_ref, k_sem)
    v_copy = pltpu.make_async_copy(v_hbm, v_ref, v_sem)
    q_copy = pltpu.make_async_copy(q_hbm, q_ref, q_sem)
    w_copy = pltpu.make_async_copy(w_hbm, w, w_sem)
    my_rows = pl.ds(pl.multiple_of(my_t * rows_t, 16), rows_t)
    cot_copy = pltpu.make_async_copy(cot_hbm, cot.at[my_rows], cot_sem)
    k_copy.start()
    v_copy.start()
    q_copy.start()
    w_copy.start()
    cot_copy.start()

    row_id = lax.broadcasted_iota(jnp.int32, (tok, tok), 0)
    col_id = lax.broadcasted_iota(jnp.int32, (tok, tok), 1)
    ld = ld_ref[...]
    highest = lax.Precision.HIGHEST
    tri = jnp.where(col_id <= row_id, 1.0, 0.0)
    cumcol = mm(tri, ld, NT, highest)
    top = lax.broadcasted_iota(jnp.int32, (16, hd), 0) < 8
    for h in range(heads):
        cum_h = cumcol[:, h : h + 1]
        end_h = cum_h[tok - 1 : tok]
        kscale[h] = jnp.broadcast_to(jnp.exp(end_h - cum_h), (tok, hd))
        g = jnp.broadcast_to(jnp.exp(end_h), (16, hd))
        high = g.astype(BF16).astype(F32)
        extra = jnp.where(top, high, g - high).astype(BF16)
        for r in range(per_head):
            send_s[h * per_head + r, piece:, :] = extra

    k_copy.wait()
    v_copy.wait()

    def state_step(h, cols):
        kp = jnp.maximum(k_ref[:, cols], 0).astype(F32)
        dec = (kscale[h] * kp).astype(BF16)
        decayed[:, cols] = dec
        state = mm(dec, v_ref[:, cols], TN).astype(BF16)
        for r in range(per_head):
            send_s[h * per_head + r, :piece, :] = state[r * piece : (r + 1) * piece]

    some_heads(state_step, 0, heads)
    pl.semaphore_wait(barrier, group + nt - 1)

    def to_owner(src, dst, ss, rs, k):
        return pltpu.make_async_remote_copy(
            src.at[slot(other(k))], dst.at[place], ss.at[k], rs.at[k],
            device_id={"tm": base + other(k)}, device_id_type=MESH)

    def from_any(src, dst, ss, rs, k):
        return pltpu.make_async_remote_copy(
            src.at[0], dst.at[source(k)], ss.at[k], rs.at[k],
            device_id={"tm": base + other(k)}, device_id_type=MESH)

    def to_any(src, dst, ss, rs, k):
        return pltpu.make_async_remote_copy(
            src.at[other(k)], dst.at[slot(place)], ss.at[k], rs.at[k],
            device_id={"tm": base + other(k)}, device_id_type=MESH)

    def from_owner(src, dst, ss, rs, k):
        return pltpu.make_async_remote_copy(
            src.at[0], dst.at[slot(source(k))], ss.at[k], rs.at[k],
            device_id={"tm": base + other(k)}, device_id_type=MESH)

    def gather_start(*way):
        partners(lambda k: owner_only(other(k), lambda: to_owner(*way, k).start()))

        def keep():
            way[1][place] = way[0][slot(place)]

        owner_only(place, keep)

    def gather_wait(*way):
        owner_only(place, lambda: partners(lambda k: from_any(*way, k).wait_recv()))

    def spread_start(*way):
        def go():
            partners(lambda k: to_any(*way, k).start())
            way[1][slot(place)] = way[0][place]

        owner_only(place, go)

    def spread_wait(*way):
        partners(lambda k: owner_only(source(k), lambda: from_owner(*way, k).wait_recv()))

    def sends_wait(way_g, way_s):
        partners(lambda k: owner_only(other(k), lambda: to_owner(*way_g, k).wait_send()))
        owner_only(place, lambda: partners(lambda k: to_any(*way_s, k).wait_send()))

    fwd_g = (send_s, recv_s, s_send, s_recv)
    fwd_s = (send_p, prefix, p_send, p_recv)
    bwd_g = (send_g, recv_g, g_send, g_recv)
    bwd_s = (send_l, later, l_send, l_recv)

    def total_copy(src, dst, ss, rs):
        return pltpu.make_async_remote_copy(
            src, dst, ss, rs, device_id={"tm": peer}, device_id_type=MESH)

    fwd_t = (send_t, recv_t, t_send, t_recv)
    bwd_t = (send_u, recv_u, u_send, u_recv)

    gather_start(*fwd_g)

    def cot_remote(k):
        return pltpu.make_async_remote_copy(
            cot_hbm, cot.at[my_rows], c_send.at[k], c_recv.at[k],
            device_id={"tensor": lax.rem(my_t + k, nt)}, device_id_type=MESH)

    def cot_arrival(k):
        s = lax.rem(my_t + nt - k, nt)
        return pltpu.make_async_remote_copy(
            cot_hbm, cot.at[pl.ds(pl.multiple_of(s * rows_t, 16), rows_t)],
            c_send.at[k], c_recv.at[k],
            device_id={"tensor": lax.rem(my_t + k, nt)}, device_id_type=MESH)

    partners(lambda k: cot_remote(k).start(), 1, nt)

    sid_row = jnp.broadcast_to(sid_ref[...].reshape(1, tok).astype(F32), (tok, tok))
    sid_col = jnp.sum(jnp.where(row_id == col_id, sid_row, 0.0), axis=1, keepdims=True)
    visible = sid_row <= sid_col
    bound[...] = jnp.where(visible, 0.0, -1e30)
    cumrow[...] = mm(ld, tri, NT, highest)
    cendcol = mm(jnp.where(visible, 1.0, 0.0), ld, NT, highest)
    for h in range(heads):
        end_b = jnp.broadcast_to(cendcol[:, h : h + 1], (tok, hd))
        ends[h] = end_b
        escale[h] = jnp.exp(end_b)
    q_copy.wait()

    def inner_step(h, cols):
        qp = jnp.maximum(q_ref[:, cols], 0)
        kp = jnp.maximum(k_ref[:, cols], 0)
        end = jnp.concatenate([ends[h]] * (tok // hd), axis=1)
        weight = jnp.exp(jnp.minimum(end - cumrow[pl.ds(h, 1), :], bound[...]))
        weights[h] = weight
        p = (weight * mm(qp, kp, NT)).astype(BF16)
        probs[h] = p
        local[:, cols] = mm(p, v_ref[:, cols], NN)

    half, most = heads // 2, 3 * heads // 4
    some_heads(inner_step, 0, half)

    gather_wait(*fwd_g)

    def scan_forward(state):
        def step(b, state):
            send_p[b] = state.astype(BF16)
            got = recv_s[b].astype(F32)
            g = got[piece : piece + 1] + got[piece + 8 : piece + 9]
            decays[pl.ds(b, 1), :] = g
            return g * state + got[:piece]

        return lax.fori_loop(0, group, step, state)

    def first_forward():
        def go():
            send_t[...] = scan_forward(jnp.zeros((piece, hd), F32)).astype(BF16)
            total_copy(*fwd_t).start()

        owner_only(place, go)
        spread_start(*fwd_s)

    def second_forward():
        def go():
            total_copy(*fwd_t).wait_recv()
            scan_forward(recv_t[...].astype(F32))

        owner_only(place, go)
        spread_start(*fwd_s)

    pl.when(jnp.logical_not(upper))(first_forward)
    some_heads(inner_step, half, most)
    pl.when(upper)(second_forward)
    some_heads(inner_step, most, heads)

    w_copy.wait()
    cot_copy.wait()
    partners(lambda k: cot_arrival(k).wait_recv(), 1, nt)
    chunk = 2 * hd if heads % 2 == 0 else hd

    def outgrad_step(c, carry):
        part = pl.ds(pl.multiple_of(c * chunk, chunk), chunk)
        outgrad[:, part] = mm(cot[...], w[part, :], NT)
        return carry

    lax.fori_loop(0, heads * hd // chunk, outgrad_step, 0)

    spread_wait(*fwd_s)

    def head_rows(buffer, h):
        parts = [buffer[h * per_head + r] for r in range(per_head)]
        return parts[0] if per_head == 1 else jnp.concatenate(parts, axis=0)

    def norm_step(h, cols):
        qp = jnp.maximum(q_ref[:, cols], 0)
        es = escale[h]
        mixed = local[:, cols] + es * mm(qp, head_rows(prefix, h), NN)
        inv = lax.rsqrt(jnp.mean(mixed * mixed, axis=1, keepdims=True) + EPSILON)
        gain = gain_ref[:, cols]
        attended[:, cols] = (mixed * inv * gain).astype(BF16)
        gained = outgrad[:, cols] * gain
        along = jnp.mean(mixed * gained, axis=1, keepdims=True)
        mg = (inv * gained - mixed * (inv * inv * inv * along)).astype(BF16)
        mixgrad[:, cols] = mg
        sq = (es * qp.astype(F32)).astype(BF16)
        grad = mm(sq, mg, TN).astype(BF16)
        for r in range(per_head):
            send_g[h * per_head + r] = grad[r * piece : (r + 1) * piece]

    some_heads(norm_step, 0, heads)
    gather_start(*bwd_g)

    step_cols = 512

    def project(c, carry):
        part = pl.ds(pl.multiple_of(c * step_cols, step_cols), step_cols)
        part_o[:, part] = mm(attended[...], w[:, part], NN).astype(BF16)
        return carry

    lax.fori_loop(0, wide // step_cols, project, 0)

    def out_copy(k):
        d = lax.rem(my_t + k, nt)
        return pltpu.make_async_remote_copy(
            part_o.at[pl.ds(pl.multiple_of(d * rows_t, 16), rows_t)], recv_o.at[k - 1],
            o_send.at[k], o_recv.at[k], device_id={"tensor": d}, device_id_type=MESH)

    partners(lambda k: out_copy(k).start(), 1, nt)

    gather_wait(*bwd_g)

    def scan_backward(state):
        def step(i, state):
            b = group - 1 - i
            send_l[b] = state.astype(BF16)
            return decays[pl.ds(b, 1), :] * state + recv_g[b].astype(F32)

        return lax.fori_loop(0, group, step, state)

    def first_backward():
        def go():
            send_u[...] = scan_backward(jnp.zeros((piece, hd), F32)).astype(BF16)
            total_copy(*bwd_t).start()

        owner_only(place, go)
        spread_start(*bwd_s)

    def second_backward():
        def go():
            total_copy(*bwd_t).wait_recv()
            scan_backward(recv_u[...].astype(F32))

        owner_only(place, go)
        spread_start(*bwd_s)

    def grad_step(h, cols):
        qp = jnp.maximum(q_ref[:, cols], 0)
        kp = jnp.maximum(k_ref[:, cols], 0)
        mg = mixgrad[:, cols]
        sg = (weights[h] * mm(mg, v_ref[:, cols], NT)).astype(BF16)
        vlocal[:, cols] = mm(probs[h], mg, TN)
        klocal[:, cols] = mm(sg, qp, TN)
        qg = mm(sg, kp, NN) + escale[h] * mm(mg, head_rows(prefix, h), NT)
        qg_ref[:, cols] = jnp.where(qp.astype(F32) > 0, qg, 0.0).astype(BF16)

    early = heads // 4
    pl.when(upper)(first_backward)
    some_heads(grad_step, 0, early)
    pl.when(jnp.logical_not(upper))(second_backward)
    some_heads(grad_step, early, heads)

    partners(lambda k: out_copy(k).wait_recv(), 1, nt)

    def total_out(c, carry):
        part = pl.ds(pl.multiple_of(c * step_cols, step_cols), step_cols)
        total = part_o[my_rows, part].astype(F32)
        for k in range(1, nt):
            total += recv_o[k - 1, :, part].astype(F32)
        out_ref[:, part] = total.astype(BF16)
        return carry

    lax.fori_loop(0, wide // step_cols, total_out, 0)

    spread_wait(*bwd_s)

    def last_step(h, cols):
        lat = head_rows(later, h)
        vg_ref[:, cols] = (vlocal[:, cols] + mm(decayed[:, cols], lat, NN)).astype(BF16)
        kg = klocal[:, cols] + kscale[h] * mm(v_ref[:, cols], lat, NT)
        kg_ref[:, cols] = jnp.where(k_ref[:, cols].astype(F32) > 0, kg, 0.0).astype(BF16)

    some_heads(last_step, 0, heads)

    partners(lambda k: cot_remote(k).wait_send(), 1, nt)
    partners(lambda k: out_copy(k).wait_send(), 1, nt)
    sends_wait(fwd_g, fwd_s)
    sends_wait(bwd_g, bwd_s)
    pl.when(jnp.logical_not(upper))(
        lambda: owner_only(place, lambda: total_copy(*fwd_t).wait_send()))
    pl.when(upper)(lambda: owner_only(place, lambda: total_copy(*bwd_t).wait_send()))


def write_kernel(*refs):
    count = (len(refs) - 1) // 2
    sems = refs[-1]
    copies = [
        pltpu.make_async_copy(refs[i], refs[count + i], sems.at[i]) for i in range(count)
    ]
    for copy in copies:
        copy.start()
    for copy in copies:
        copy.wait()


def on_device(n, nt, q, k, v, ld, sid, gain, w, cot):
    tok, width = q.shape
    heads = ld.shape[0]
    hd = width // heads
    wide = w.shape[1]
    rows_t = cot.shape[0]
    group = n // 2
    owners = owners_of(width, hd, group)
    piece = width // owners
    vmem = pl.BlockSpec(memory_space=pltpu.VMEM)
    hbm = pl.BlockSpec(memory_space=pl.ANY)
    dma = pltpu.SemaphoreType.DMA
    flat16 = pltpu.VMEM((tok, width), BF16)
    flat32 = pltpu.VMEM((tok, width), F32)
    wide_h = pltpu.VMEM((heads, tok, hd), F32)
    one = pltpu.VMEM((piece, hd), BF16)
    by_owner = pltpu.VMEM((owners, piece, hd), BF16)
    by_place = pltpu.VMEM((group, piece, hd), BF16)
    shapes = ((rows_t, wide), (tok, width), (tok, width), (tok, width))
    cost = pl.CostEstimate(
        flops=4 * tok * width * wide + 14 * tok * tok * width + 12 * tok * width * hd,
        bytes_accessed=2 * width * wide + 16 * tok * width,
        transcendentals=heads * tok * tok,
    )
    results = pl.pallas_call(
        functools.partial(kernel, n, nt, owners),
        out_shape=tuple(pltpu.VMEM(shape, BF16) for shape in shapes),
        in_specs=[vmem] * 3 + [hbm] * 5,
        out_specs=(vmem,) * 4,
        scratch_shapes=[
            flat16, flat16, flat16,
            pltpu.VMEM(w.shape, BF16),
            pltpu.VMEM((tok, wide), BF16),
            pltpu.VMEM((tok, tok), F32),
            pltpu.VMEM((heads, tok), F32),
            wide_h, wide_h, wide_h,
            flat16,
            pltpu.VMEM((heads, tok, tok), F32),
            pltpu.VMEM((heads, tok, tok), BF16),
            flat32, flat32, flat16, flat16, flat32, flat32,
            pltpu.VMEM((group, hd), F32),
            pltpu.VMEM((owners, piece + 16, hd), BF16),
            pltpu.VMEM((group, piece + 16, hd), BF16),
            by_place, by_owner, by_owner, by_place, by_place, by_owner,
            one, one, one, one,
            pltpu.VMEM((tok, wide), BF16),
            pltpu.VMEM((max(nt - 1, 1), rows_t, wide), BF16),
            dma, dma, dma, dma, dma, dma((nt,)), dma((nt,)),
            dma((group,)), dma((group,)), dma((group,)), dma((group,)),
            dma((group,)), dma((group,)), dma((group,)), dma((group,)),
            dma((nt,)), dma((nt,)), dma, dma, dma, dma,
        ],
        compiler_params=pltpu.CompilerParams(
            collective_id=0, has_side_effects=True, vmem_limit_bytes=50 * 1024 * 1024
        ),
        cost_estimate=cost,
    )(ld, sid, gain.reshape(1, -1), q, k, v, w, cot)
    return pl.pallas_call(
        write_kernel,
        out_shape=tuple(jax.ShapeDtypeStruct(shape, BF16) for shape in shapes),
        in_specs=[vmem] * 4,
        out_specs=(hbm,) * 4,
        scratch_shapes=[dma((4,))],
    )(*results)


def solution(mesh):
    n, nt = mesh.shape["tm"], mesh.shape["tensor"]
    return jax.shard_map(
        functools.partial(on_device, n, nt),
        mesh=mesh,
        in_specs=(
            P("tm", "tensor"),
            P("tm", "tensor"),
            P("tm", "tensor"),
            P("tensor", "tm"),
            P("tm"),
            P("tensor"),
            P("tensor", None),
            P(("tm", "tensor"), None),
        ),
        out_specs=(
            P(("tm", "tensor"), None),
            P("tm", "tensor"),
            P("tm", "tensor"),
            P("tm", "tensor"),
        ),
        check_vma=False,
    )
```

```python
import functools

import jax
import jax.numpy as jnp
from jax import lax
from jax.experimental import pallas as pl
from jax.experimental.pallas import tpu as pltpu
from jax.sharding import PartitionSpec as P

EPSILON = 1e-06
F32 = jnp.float32
BF16 = jnp.bfloat16
MESH = pl.DeviceIdType.MESH
NT = (((1,), (1,)), ((), ()))
TN = (((0,), (0,)), ((), ()))
NN = (((1,), (0,)), ((), ()))


def mm(a, b, dims, precision=None):
    return lax.dot_general(a, b, dims, precision=precision, preferred_element_type=F32)


def owners_of(rows, head_size, count):
    owners = count
    while rows % owners or (rows // owners) % 16 or head_size % (rows // owners):
        owners -= 1
    return owners


def kernel(
    n, nt, owners,
    ld_hbm, sid_hbm, gain_hbm, q_hbm, k_hbm, v_hbm, w_hbm, cot_hbm,
    out_ref, qg_ref, kg_ref, vg_ref,
    ld_ref, sid_ref, gain_ref, q_ref, k_ref, v_ref, w, cot, bound, cumrow, kscale, ends, escale, decayed, weights, probs,
    local, outgrad, attended, mixgrad, vlocal, klocal, decays,
    send_s, recv_s, send_p, prefix, send_g, recv_g, send_l, later,
    send_t, recv_t, send_u, recv_u, part_o, recv_o,
    small_sem, w_sem, cot_sem, q_sem, k_sem, v_sem, c_send, c_recv, s_send, s_recv, p_send, p_recv,
    g_send, g_recv, l_send, l_recv, o_send, o_recv, t_send, t_recv, u_send, u_recv,
):
    group = n // 2
    me = lax.axis_index("tm")
    my_t = lax.axis_index("tensor")
    upper = me >= group
    base = (me // group) * group
    place = me - base
    peer = lax.rem(me + group, n)
    tok = q_ref.shape[0]
    heads = ld_ref.shape[0]
    hd = q_ref.shape[1] // heads
    rows_t = tok // nt
    piece = heads * hd // owners
    per_head = owners // heads
    wide = w.shape[1]
    direct = owners == group and per_head == 1 and group % 2 == 0

    def other(k):
        return lax.rem(place + k, group)

    def source(k):
        return lax.rem(place + group - k, group)

    def owner_only(index, body):
        if owners == group:
            body()
        else:
            pl.when(index < owners)(body)

    def slot(index):
        return index if owners == group else jnp.minimum(index, owners - 1)

    def partners(body, lowest=1, count=group):
        def step(k, carry):
            body(k)
            return carry

        lax.fori_loop(lowest, count, step, 0)

    def some_heads(body, low, high):
        width = 2 if (high - low) % 2 == 0 else 1

        def step(i, carry):
            for u in range(width):
                h = low + i * width + u
                body(h, pl.ds(pl.multiple_of(h * hd, hd), hd))
            return carry

        lax.fori_loop(0, (high - low) // width, step, 0)

    barrier = pltpu.get_barrier_semaphore()
    partners(lambda k: pl.semaphore_signal(
        barrier, inc=1, device_id={"tm": base + other(k)}, device_id_type=MESH))
    pl.semaphore_signal(barrier, inc=1, device_id={"tm": peer}, device_id_type=MESH)
    partners(lambda k: pl.semaphore_signal(
        barrier, inc=1, device_id={"tensor": lax.rem(my_t + k, nt)}, device_id_type=MESH), 1, nt)

    small = [
        pltpu.make_async_copy(src, dst, small_sem.at[i])
        for i, (src, dst) in enumerate(
            ((ld_hbm, ld_ref), (sid_hbm, sid_ref), (gain_hbm, gain_ref)))
    ]
    small[0].start()
    k_copy = pltpu.make_async_copy(k_hbm, k_ref, k_sem)
    v_copy = pltpu.make_async_copy(v_hbm, v_ref, v_sem)
    q_copy = pltpu.make_async_copy(q_hbm, q_ref, q_sem)
    w_copy = pltpu.make_async_copy(w_hbm, w, w_sem)
    my_rows = pl.ds(pl.multiple_of(my_t * rows_t, 16), rows_t)
    cot_copy = pltpu.make_async_copy(cot_hbm, cot.at[my_rows], cot_sem)
    k_copy.start()
    v_copy.start()
    small[1].start()
    small[2].start()
    q_copy.start()
    w_copy.start()
    cot_copy.start()

    row_id = lax.broadcasted_iota(jnp.int32, (tok, tok), 0)
    col_id = lax.broadcasted_iota(jnp.int32, (tok, tok), 1)
    highest = lax.Precision.HIGHEST
    tri = jnp.where(col_id <= row_id, 1.0, 0.0)
    small[0].wait()
    ld = ld_ref[...]
    cumcol = mm(tri, ld, NT, highest)
    top = lax.broadcasted_iota(jnp.int32, (16, hd), 0) < 8
    for h in range(heads):
        cum_h = cumcol[:, h : h + 1]
        end_h = cum_h[tok - 1 : tok]
        kscale[h] = jnp.broadcast_to(jnp.exp(end_h - cum_h), (tok, hd))
        g = jnp.broadcast_to(jnp.exp(end_h), (16, hd))
        high = g.astype(BF16).astype(F32)
        extra = jnp.where(top, high, g - high).astype(BF16)
        for r in range(per_head):
            send_s[h * per_head + r, piece:, :] = extra

    k_copy.wait()
    v_copy.wait()

    def state_step(h, cols):
        kp = jnp.maximum(k_ref[:, cols], 0).astype(F32)
        dec = (kscale[h] * kp).astype(BF16)
        decayed[:, cols] = dec
        state = mm(dec, v_ref[:, cols], TN).astype(BF16)
        for r in range(per_head):
            send_s[h * per_head + r, :piece, :] = state[r * piece : (r + 1) * piece]

    if not direct:
        some_heads(state_step, 0, heads)
    pl.semaphore_wait(barrier, group + nt - 1)

    def to_owner(src, dst, ss, rs, k):
        return pltpu.make_async_remote_copy(
            src.at[slot(other(k))], dst.at[place], ss.at[k], rs.at[k],
            device_id={"tm": base + other(k)}, device_id_type=MESH)

    def from_any(src, dst, ss, rs, k):
        return pltpu.make_async_remote_copy(
            src.at[0], dst.at[source(k)], ss.at[k], rs.at[k],
            device_id={"tm": base + other(k)}, device_id_type=MESH)

    def to_any(src, dst, ss, rs, k):
        return pltpu.make_async_remote_copy(
            src.at[other(k)], dst.at[slot(place)], ss.at[k], rs.at[k],
            device_id={"tm": base + other(k)}, device_id_type=MESH)

    def from_owner(src, dst, ss, rs, k):
        return pltpu.make_async_remote_copy(
            src.at[0], dst.at[slot(source(k))], ss.at[k], rs.at[k],
            device_id={"tm": base + other(k)}, device_id_type=MESH)

    def gather_start(*way):
        partners(lambda k: owner_only(other(k), lambda: to_owner(*way, k).start()))

        def keep():
            way[1][place] = way[0][slot(place)]

        owner_only(place, keep)

    def gather_wait(*way):
        owner_only(place, lambda: partners(lambda k: from_any(*way, k).wait_recv()))

    def spread_start(*way):
        def go():
            partners(lambda k: to_any(*way, k).start())
            way[1][slot(place)] = way[0][place]

        owner_only(place, go)

    def spread_wait(*way):
        partners(lambda k: owner_only(source(k), lambda: from_owner(*way, k).wait_recv()))

    def sends_wait(way_g, way_s):
        partners(lambda k: owner_only(other(k), lambda: to_owner(*way_g, k).wait_send()))
        owner_only(place, lambda: partners(lambda k: to_any(*way_s, k).wait_send()))

    fwd_g = (send_s, recv_s, s_send, s_recv)
    fwd_s = (send_p, prefix, p_send, p_recv)
    bwd_g = (send_g, recv_g, g_send, g_recv)
    bwd_s = (send_l, later, l_send, l_recv)

    def total_copy(src, dst, ss, rs):
        return pltpu.make_async_remote_copy(
            src, dst, ss, rs, device_id={"tm": peer}, device_id_type=MESH)

    fwd_t = (send_t, recv_t, t_send, t_recv)
    bwd_t = (send_u, recv_u, u_send, u_recv)

    def columns(h):
        return pl.ds(pl.multiple_of(h * hd, hd), hd)

    def keep_mine(src, dst, *_):
        dst[place] = src[place]

    if direct:
        def state_pair(i, carry):
            k = 2 * i + 1
            state_step(other(k), columns(other(k)))
            state_step(other(k + 1), columns(other(k + 1)))
            to_owner(*fwd_g, k).start()
            to_owner(*fwd_g, k + 1).start()
            return carry

        lax.fori_loop(0, group // 2 - 1, state_pair, 0)
        state_step(other(group - 1), columns(other(group - 1)))
        state_step(place, columns(place))
        to_owner(*fwd_g, group - 1).start()
        keep_mine(*fwd_g)
    else:
        gather_start(*fwd_g)

    def cot_remote(k):
        return pltpu.make_async_remote_copy(
            cot_hbm, cot.at[my_rows], c_send.at[k], c_recv.at[k],
            device_id={"tensor": lax.rem(my_t + k, nt)}, device_id_type=MESH)

    def cot_arrival(k):
        s = lax.rem(my_t + nt - k, nt)
        return pltpu.make_async_remote_copy(
            cot_hbm, cot.at[pl.ds(pl.multiple_of(s * rows_t, 16), rows_t)],
            c_send.at[k], c_recv.at[k],
            device_id={"tensor": lax.rem(my_t + k, nt)}, device_id_type=MESH)

    partners(lambda k: cot_remote(k).start(), 1, nt)

    small[1].wait()
    small[2].wait()
    sid_row = jnp.broadcast_to(sid_ref[...].reshape(1, tok).astype(F32), (tok, tok))
    sid_col = jnp.sum(jnp.where(row_id == col_id, sid_row, 0.0), axis=1, keepdims=True)
    visible = sid_row <= sid_col
    bound[...] = jnp.where(visible, 0.0, -1e30)
    cumrow[...] = mm(ld, tri, NT, highest)
    cendcol = mm(jnp.where(visible, 1.0, 0.0), ld, NT, highest)
    for h in range(heads):
        end_b = jnp.broadcast_to(cendcol[:, h : h + 1], (tok, hd))
        ends[h] = end_b
        escale[h] = jnp.exp(end_b)
    q_copy.wait()

    def inner_step(h, cols):
        qp = jnp.maximum(q_ref[:, cols], 0)
        kp = jnp.maximum(k_ref[:, cols], 0)
        end = jnp.concatenate([ends[h]] * (tok // hd), axis=1)
        weight = jnp.exp(jnp.minimum(end - cumrow[pl.ds(h, 1), :], bound[...]))
        weights[h] = weight
        p = (weight * mm(qp, kp, NT)).astype(BF16)
        probs[h] = p
        local[:, cols] = mm(p, v_ref[:, cols], NN)

    half, most = heads // 4, 3 * heads // 4
    some_heads(inner_step, 0, half)

    gather_wait(*fwd_g)

    def scan_forward(state):
        def step(b, state):
            send_p[b] = state.astype(BF16)
            got = recv_s[b].astype(F32)
            g = got[piece : piece + 1] + got[piece + 8 : piece + 9]
            decays[pl.ds(b, 1), :] = g
            return g * state + got[:piece]

        return lax.fori_loop(0, group, step, state)

    def first_forward():
        def go():
            send_t[...] = scan_forward(jnp.zeros((piece, hd), F32)).astype(BF16)
            total_copy(*fwd_t).start()

        owner_only(place, go)
        spread_start(*fwd_s)

    def second_forward():
        def go():
            total_copy(*fwd_t).wait_recv()
            scan_forward(recv_t[...].astype(F32))

        owner_only(place, go)
        spread_start(*fwd_s)

    pl.when(jnp.logical_not(upper))(first_forward)
    some_heads(inner_step, half, most)
    pl.when(upper)(second_forward)
    some_heads(inner_step, most, heads)

    w_copy.wait()
    cot_copy.wait()
    partners(lambda k: cot_arrival(k).wait_recv(), 1, nt)
    chunk = 2 * hd if heads % 2 == 0 else hd

    def outgrad_step(c, carry):
        part = pl.ds(pl.multiple_of(c * chunk, chunk), chunk)
        outgrad[:, part] = mm(cot[...], w[part, :], NT)
        return carry

    lax.fori_loop(0, heads * hd // chunk, outgrad_step, 0)

    def head_rows(buffer, h):
        parts = [buffer[h * per_head + r] for r in range(per_head)]
        return parts[0] if per_head == 1 else jnp.concatenate(parts, axis=0)

    def norm_step(h, cols):
        qp = jnp.maximum(q_ref[:, cols], 0)
        es = escale[h]
        mixed = local[:, cols] + es * mm(qp, head_rows(prefix, h), NN)
        inv = lax.rsqrt(jnp.mean(mixed * mixed, axis=1, keepdims=True) + EPSILON)
        gain = gain_ref[:, cols]
        attended[:, cols] = (mixed * inv * gain).astype(BF16)
        gained = outgrad[:, cols] * gain
        along = jnp.mean(mixed * gained, axis=1, keepdims=True)
        mg = (inv * gained - mixed * (inv * inv * inv * along)).astype(BF16)
        mixgrad[:, cols] = mg
        sq = (es * qp.astype(F32)).astype(BF16)
        grad = mm(sq, mg, TN).astype(BF16)
        for r in range(per_head):
            send_g[h * per_head + r] = grad[r * piece : (r + 1) * piece]

    if direct:
        norm_step(place, columns(place))
        from_owner(*fwd_s, 1).wait_recv()
        norm_step(source(1), columns(source(1)))
        to_owner(*bwd_g, group - 1).start()

        def norm_pair(i, carry):
            k = 2 * i
            from_owner(*fwd_s, k).wait_recv()
            from_owner(*fwd_s, k + 1).wait_recv()
            norm_step(source(k), columns(source(k)))
            norm_step(source(k + 1), columns(source(k + 1)))
            to_owner(*bwd_g, group - k).start()
            to_owner(*bwd_g, group - k - 1).start()
            return carry

        lax.fori_loop(1, group // 2, norm_pair, 0)
        keep_mine(*bwd_g)
    else:
        spread_wait(*fwd_s)
        some_heads(norm_step, 0, heads)
        gather_start(*bwd_g)

    step_cols = 512

    def project(c, carry):
        part = pl.ds(pl.multiple_of(c * step_cols, step_cols), step_cols)
        part_o[:, part] = mm(attended[...], w[:, part], NN).astype(BF16)
        return carry

    half_cols = wide // step_cols // 2
    lax.fori_loop(0, half_cols, project, 0)

    def out_copy(k):
        d = lax.rem(my_t + k, nt)
        return pltpu.make_async_remote_copy(
            part_o.at[pl.ds(pl.multiple_of(d * rows_t, 16), rows_t)], recv_o.at[k - 1],
            o_send.at[k], o_recv.at[k], device_id={"tensor": d}, device_id_type=MESH)

    gather_wait(*bwd_g)

    def scan_backward(state):
        def step(i, state):
            b = group - 1 - i
            send_l[b] = state.astype(BF16)
            return decays[pl.ds(b, 1), :] * state + recv_g[b].astype(F32)

        return lax.fori_loop(0, group, step, state)

    def first_backward():
        def go():
            send_u[...] = scan_backward(jnp.zeros((piece, hd), F32)).astype(BF16)
            total_copy(*bwd_t).start()

        owner_only(place, go)
        spread_start(*bwd_s)

    def second_backward():
        def go():
            total_copy(*bwd_t).wait_recv()
            scan_backward(recv_u[...].astype(F32))

        owner_only(place, go)
        spread_start(*bwd_s)

    def grad_step(h, cols):
        qp = jnp.maximum(q_ref[:, cols], 0)
        kp = jnp.maximum(k_ref[:, cols], 0)
        mg = mixgrad[:, cols]
        sg = (weights[h] * mm(mg, v_ref[:, cols], NT)).astype(BF16)
        vlocal[:, cols] = mm(probs[h], mg, TN)
        klocal[:, cols] = mm(sg, qp, TN)
        qg = mm(sg, kp, NN) + escale[h] * mm(mg, head_rows(prefix, h), NT)
        qg_ref[:, cols] = jnp.where(qp.astype(F32) > 0, qg, 0.0).astype(BF16)

    early = heads // 2
    pl.when(upper)(first_backward)
    lax.fori_loop(half_cols, wide // step_cols, project, 0)
    partners(lambda k: out_copy(k).start(), 1, nt)
    some_heads(grad_step, 0, early)
    pl.when(jnp.logical_not(upper))(second_backward)
    some_heads(grad_step, early, heads)

    partners(lambda k: out_copy(k).wait_recv(), 1, nt)

    def total_out(c, carry):
        part = pl.ds(pl.multiple_of(c * step_cols, step_cols), step_cols)
        total = part_o[my_rows, part].astype(F32)
        for k in range(1, nt):
            total += recv_o[k - 1, :, part].astype(F32)
        out_ref[:, part] = total.astype(BF16)
        return carry

    lax.fori_loop(0, wide // step_cols, total_out, 0)

    def last_step(h, cols):
        lat = head_rows(later, h)
        vg_ref[:, cols] = (vlocal[:, cols] + mm(decayed[:, cols], lat, NN)).astype(BF16)
        kg = klocal[:, cols] + kscale[h] * mm(v_ref[:, cols], lat, NT)
        kg_ref[:, cols] = jnp.where(k_ref[:, cols].astype(F32) > 0, kg, 0.0).astype(BF16)

    if direct:
        last_step(place, columns(place))
        from_owner(*bwd_s, 1).wait_recv()
        last_step(source(1), columns(source(1)))

        def last_pair(i, carry):
            k = 2 * i
            from_owner(*bwd_s, k).wait_recv()
            from_owner(*bwd_s, k + 1).wait_recv()
            last_step(source(k), columns(source(k)))
            last_step(source(k + 1), columns(source(k + 1)))
            return carry

        lax.fori_loop(1, group // 2, last_pair, 0)
    else:
        spread_wait(*bwd_s)
        some_heads(last_step, 0, heads)

    partners(lambda k: cot_remote(k).wait_send(), 1, nt)
    partners(lambda k: out_copy(k).wait_send(), 1, nt)
    sends_wait(fwd_g, fwd_s)
    sends_wait(bwd_g, bwd_s)
    pl.when(jnp.logical_not(upper))(
        lambda: owner_only(place, lambda: total_copy(*fwd_t).wait_send()))
    pl.when(upper)(lambda: owner_only(place, lambda: total_copy(*bwd_t).wait_send()))


def write_kernel(*refs):
    count = (len(refs) - 1) // 2
    sems = refs[-1]
    copies = [
        pltpu.make_async_copy(refs[i], refs[count + i], sems.at[i]) for i in range(count)
    ]
    for copy in copies:
        copy.start()
    for copy in copies:
        copy.wait()


def on_device(n, nt, q, k, v, ld, sid, gain, w, cot):
    tok, width = q.shape
    heads = ld.shape[0]
    hd = width // heads
    wide = w.shape[1]
    rows_t = cot.shape[0]
    group = n // 2
    owners = owners_of(width, hd, group)
    piece = width // owners
    vmem = pl.BlockSpec(memory_space=pltpu.VMEM)
    hbm = pl.BlockSpec(memory_space=pl.ANY)
    dma = pltpu.SemaphoreType.DMA
    flat16 = pltpu.VMEM((tok, width), BF16)
    flat32 = pltpu.VMEM((tok, width), F32)
    wide_h = pltpu.VMEM((heads, tok, hd), F32)
    one = pltpu.VMEM((piece, hd), BF16)
    by_owner = pltpu.VMEM((owners, piece, hd), BF16)
    by_place = pltpu.VMEM((group, piece, hd), BF16)
    shapes = ((rows_t, wide), (tok, width), (tok, width), (tok, width))
    cost = pl.CostEstimate(
        flops=4 * tok * width * wide + 14 * tok * tok * width + 12 * tok * width * hd,
        bytes_accessed=2 * width * wide + 16 * tok * width,
        transcendentals=heads * tok * tok,
    )
    args = [
        pltpu.with_memory_space_constraint(x, pltpu.HBM)
        for x in (ld, sid, gain.reshape(1, -1), q, k, v, w, cot)
    ]
    results = pl.pallas_call(
        functools.partial(kernel, n, nt, owners),
        out_shape=tuple(pltpu.VMEM(shape, BF16) for shape in shapes),
        in_specs=[pl.BlockSpec(memory_space=pltpu.HBM)] * 8,
        out_specs=(vmem,) * 4,
        scratch_shapes=[
            pltpu.VMEM(ld.shape, F32),
            pltpu.VMEM(sid.shape, jnp.int32),
            pltpu.VMEM((1, width), F32),
            flat16, flat16, flat16,
            pltpu.VMEM(w.shape, BF16),
            pltpu.VMEM((tok, wide), BF16),
            pltpu.VMEM((tok, tok), F32),
            pltpu.VMEM((heads, tok), F32),
            wide_h, wide_h, wide_h,
            flat16,
            pltpu.VMEM((heads, tok, tok), F32),
            pltpu.VMEM((heads, tok, tok), BF16),
            flat32, flat32, flat16, flat16, flat32, flat32,
            pltpu.VMEM((group, hd), F32),
            pltpu.VMEM((owners, piece + 16, hd), BF16),
            pltpu.VMEM((group, piece + 16, hd), BF16),
            by_place, by_owner, by_owner, by_place, by_place, by_owner,
            one, one, one, one,
            pltpu.VMEM((tok, wide), BF16),
            pltpu.VMEM((max(nt - 1, 1), rows_t, wide), BF16),
            dma((3,)), dma, dma, dma, dma, dma, dma((nt,)), dma((nt,)),
            dma((group,)), dma((group,)), dma((group,)), dma((group,)),
            dma((group,)), dma((group,)), dma((group,)), dma((group,)),
            dma((nt,)), dma((nt,)), dma, dma, dma, dma,
        ],
        compiler_params=pltpu.CompilerParams(
            collective_id=0, has_side_effects=True, vmem_limit_bytes=50 * 1024 * 1024
        ),
        cost_estimate=cost,
    )(*args)
    return pl.pallas_call(
        write_kernel,
        out_shape=tuple(jax.ShapeDtypeStruct(shape, BF16) for shape in shapes),
        in_specs=[hbm] * 4,
        out_specs=(hbm,) * 4,
        scratch_shapes=[dma((4,))],
        compiler_params=pltpu.CompilerParams(vmem_limit_bytes=2 * 1024 * 1024),
    )(*results)


def solution(mesh):
    n, nt = mesh.shape["tm"], mesh.shape["tensor"]
    return jax.shard_map(
        functools.partial(on_device, n, nt),
        mesh=mesh,
        in_specs=(
            P("tm", "tensor"),
            P("tm", "tensor"),
            P("tm", "tensor"),
            P("tensor", "tm"),
            P("tm"),
            P("tensor"),
            P("tensor", None),
            P(("tm", "tensor"), None),
        ),
        out_specs=(
            P(("tm", "tensor"), None),
            P("tm", "tensor"),
            P("tm", "tensor"),
            P("tm", "tensor"),
        ),
        check_vma=False,
    )
```

```python
import functools

import jax
import jax.numpy as jnp
from jax import lax
from jax.experimental import pallas as pl
from jax.experimental.pallas import tpu as pltpu
from jax.sharding import PartitionSpec as P

EPSILON = 1e-06
F32 = jnp.float32
BF16 = jnp.bfloat16
MESH = pl.DeviceIdType.MESH
NT = (((1,), (1,)), ((), ()))
TN = (((0,), (0,)), ((), ()))
NN = (((1,), (0,)), ((), ()))


def mm(a, b, dims, precision=None):
    return lax.dot_general(a, b, dims, precision=precision, preferred_element_type=F32)


def owners_of(rows, head_size, count):
    owners = count
    while rows % owners or (rows // owners) % 16 or head_size % (rows // owners):
        owners -= 1
    return owners


def kernel(
    n, nt, owners,
    ld_hbm, sid_hbm, gain_hbm, q_hbm, k_hbm, v_hbm, w_hbm, cot_hbm,
    out_ref, qg_ref, kg_ref, vg_ref,
    ld_ref, sid_ref, gain_ref, q_ref, k_ref, v_ref, w, cot, bound, cumrow, kscale, ends, escale, decayed, weights, probs,
    local, outgrad, attended, mixgrad, vlocal, klocal, decays,
    send_s, recv_s, send_p, prefix, send_g, recv_g, send_l, later,
    send_t, recv_t, send_u, recv_u, part_o, recv_o,
    small_sem, w_sem, cot_sem, q_sem, k_sem, v_sem, c_send, c_recv, s_send, s_recv, p_send, p_recv,
    g_send, g_recv, l_send, l_recv, o_send, o_recv, t_send, t_recv, u_send, u_recv,
):
    group = n // 2
    me = lax.axis_index("tm")
    my_t = lax.axis_index("tensor")
    upper = me >= group
    base = (me // group) * group
    place = me - base
    peer = lax.rem(me + group, n)
    tok = q_ref.shape[0]
    heads = ld_ref.shape[0]
    hd = q_ref.shape[1] // heads
    rows_t = tok // nt
    piece = heads * hd // owners
    per_head = owners // heads
    wide = w.shape[1]
    direct = owners == group and per_head == 1 and group % 2 == 0

    def other(k):
        return lax.rem(place + k, group)

    def source(k):
        return lax.rem(place + group - k, group)

    def owner_only(index, body):
        if owners == group:
            body()
        else:
            pl.when(index < owners)(body)

    def slot(index):
        return index if owners == group else jnp.minimum(index, owners - 1)

    def partners(body, lowest=1, count=group):
        def step(k, carry):
            body(k)
            return carry

        lax.fori_loop(lowest, count, step, 0)

    def some_heads(body, low, high):
        width = next(size for size in (4, 2, 1) if (high - low) % size == 0)

        def step(i, carry):
            for u in range(width):
                h = low + i * width + u
                body(h, pl.ds(pl.multiple_of(h * hd, hd), hd))
            return carry

        lax.fori_loop(0, (high - low) // width, step, 0)

    barrier = pltpu.get_barrier_semaphore()
    partners(lambda k: pl.semaphore_signal(
        barrier, inc=1, device_id={"tm": base + other(k)}, device_id_type=MESH))
    pl.semaphore_signal(barrier, inc=1, device_id={"tm": peer}, device_id_type=MESH)
    partners(lambda k: pl.semaphore_signal(
        barrier, inc=1, device_id={"tensor": lax.rem(my_t + k, nt)}, device_id_type=MESH), 1, nt)

    small = [
        pltpu.make_async_copy(src, dst, small_sem.at[i])
        for i, (src, dst) in enumerate(
            ((ld_hbm, ld_ref), (sid_hbm, sid_ref), (gain_hbm, gain_ref)))
    ]
    small[0].start()
    k_copy = pltpu.make_async_copy(k_hbm, k_ref, k_sem)
    v_copy = pltpu.make_async_copy(v_hbm, v_ref, v_sem)
    q_copy = pltpu.make_async_copy(q_hbm, q_ref, q_sem)
    w_copy = pltpu.make_async_copy(w_hbm, w, w_sem)
    my_rows = pl.ds(pl.multiple_of(my_t * rows_t, 16), rows_t)
    cot_copy = pltpu.make_async_copy(cot_hbm, cot.at[my_rows], cot_sem)
    k_copy.start()
    v_copy.start()
    small[1].start()
    small[2].start()
    q_copy.start()
    w_copy.start()
    cot_copy.start()

    row_id = lax.broadcasted_iota(jnp.int32, (tok, tok), 0)
    col_id = lax.broadcasted_iota(jnp.int32, (tok, tok), 1)
    highest = lax.Precision.HIGHEST
    tri = jnp.where(col_id <= row_id, 1.0, 0.0)
    small[0].wait()
    ld = ld_ref[...]
    cumcol = mm(tri, ld, NT, highest)
    top = lax.broadcasted_iota(jnp.int32, (16, hd), 0) < 8
    for h in range(heads):
        cum_h = cumcol[:, h : h + 1]
        end_h = cum_h[tok - 1 : tok]
        kscale[h] = jnp.broadcast_to(jnp.exp(end_h - cum_h), (tok, hd))
        g = jnp.broadcast_to(jnp.exp(end_h), (16, hd))
        high = g.astype(BF16).astype(F32)
        extra = jnp.where(top, high, g - high).astype(BF16)
        for r in range(per_head):
            send_s[h * per_head + r, piece:, :] = extra

    k_copy.wait()
    v_copy.wait()

    def state_step(h, cols):
        kp = jnp.maximum(k_ref[:, cols], 0).astype(F32)
        dec = (kscale[h] * kp).astype(BF16)
        decayed[:, cols] = dec
        state = mm(dec, v_ref[:, cols], TN).astype(BF16)
        for r in range(per_head):
            send_s[h * per_head + r, :piece, :] = state[r * piece : (r + 1) * piece]

    if not direct:
        some_heads(state_step, 0, heads)
    pl.semaphore_wait(barrier, group + nt - 1)

    def to_owner(src, dst, ss, rs, k):
        return pltpu.make_async_remote_copy(
            src.at[slot(other(k))], dst.at[place], ss.at[k], rs.at[k],
            device_id={"tm": base + other(k)}, device_id_type=MESH)

    def from_any(src, dst, ss, rs, k):
        return pltpu.make_async_remote_copy(
            src.at[0], dst.at[source(k)], ss.at[k], rs.at[k],
            device_id={"tm": base + other(k)}, device_id_type=MESH)

    def to_any(src, dst, ss, rs, k):
        return pltpu.make_async_remote_copy(
            src.at[other(k)], dst.at[slot(place)], ss.at[k], rs.at[k],
            device_id={"tm": base + other(k)}, device_id_type=MESH)

    def from_owner(src, dst, ss, rs, k):
        return pltpu.make_async_remote_copy(
            src.at[0], dst.at[slot(source(k))], ss.at[k], rs.at[k],
            device_id={"tm": base + other(k)}, device_id_type=MESH)

    def gather_start(*way):
        partners(lambda k: owner_only(other(k), lambda: to_owner(*way, k).start()))

        def keep():
            way[1][place] = way[0][slot(place)]

        owner_only(place, keep)

    def gather_wait(*way):
        owner_only(place, lambda: partners(lambda k: from_any(*way, k).wait_recv()))

    def spread_start(*way):
        def go():
            partners(lambda k: to_any(*way, k).start())
            way[1][slot(place)] = way[0][place]

        owner_only(place, go)

    def spread_wait(*way):
        partners(lambda k: owner_only(source(k), lambda: from_owner(*way, k).wait_recv()))

    def sends_wait(way_g, way_s):
        partners(lambda k: owner_only(other(k), lambda: to_owner(*way_g, k).wait_send()))
        owner_only(place, lambda: partners(lambda k: to_any(*way_s, k).wait_send()))

    fwd_g = (send_s, recv_s, s_send, s_recv)
    fwd_s = (send_p, prefix, p_send, p_recv)
    bwd_g = (send_g, recv_g, g_send, g_recv)
    bwd_s = (send_l, later, l_send, l_recv)

    def total_copy(src, dst, ss, rs):
        return pltpu.make_async_remote_copy(
            src, dst, ss, rs, device_id={"tm": peer}, device_id_type=MESH)

    fwd_t = (send_t, recv_t, t_send, t_recv)
    bwd_t = (send_u, recv_u, u_send, u_recv)

    def columns(h):
        return pl.ds(pl.multiple_of(h * hd, hd), hd)

    def keep_mine(src, dst, *_):
        dst[place] = src[place]

    if direct:
        def state_pair(i, carry):
            k = 2 * i + 1
            state_step(other(k), columns(other(k)))
            state_step(other(k + 1), columns(other(k + 1)))
            to_owner(*fwd_g, k).start()
            to_owner(*fwd_g, k + 1).start()
            return carry

        lax.fori_loop(0, group // 2 - 1, state_pair, 0)
        state_step(other(group - 1), columns(other(group - 1)))
        state_step(place, columns(place))
        to_owner(*fwd_g, group - 1).start()
        keep_mine(*fwd_g)
    else:
        gather_start(*fwd_g)

    def cot_remote(k):
        return pltpu.make_async_remote_copy(
            cot_hbm, cot.at[my_rows], c_send.at[k], c_recv.at[k],
            device_id={"tensor": lax.rem(my_t + k, nt)}, device_id_type=MESH)

    def cot_arrival(k):
        s = lax.rem(my_t + nt - k, nt)
        return pltpu.make_async_remote_copy(
            cot_hbm, cot.at[pl.ds(pl.multiple_of(s * rows_t, 16), rows_t)],
            c_send.at[k], c_recv.at[k],
            device_id={"tensor": lax.rem(my_t + k, nt)}, device_id_type=MESH)

    partners(lambda k: cot_remote(k).start(), 1, nt)

    small[1].wait()
    small[2].wait()
    sid_row = jnp.broadcast_to(sid_ref[...].reshape(1, tok).astype(F32), (tok, tok))
    sid_col = jnp.sum(jnp.where(row_id == col_id, sid_row, 0.0), axis=1, keepdims=True)
    visible = sid_row <= sid_col
    bound[...] = jnp.where(visible, 0.0, -1e30)
    cumrow[...] = mm(ld, tri, NT, highest)
    cendcol = mm(jnp.where(visible, 1.0, 0.0), ld, NT, highest)
    for h in range(heads):
        end_b = jnp.broadcast_to(cendcol[:, h : h + 1], (tok, hd))
        ends[h] = end_b
        escale[h] = jnp.exp(end_b)
    q_copy.wait()

    def inner_step(h, cols):
        qp = jnp.maximum(q_ref[:, cols], 0)
        kp = jnp.maximum(k_ref[:, cols], 0)
        end = jnp.concatenate([ends[h]] * (tok // hd), axis=1)
        weight = jnp.exp(jnp.minimum(end - cumrow[pl.ds(h, 1), :], bound[...]))
        weights[h] = weight
        p = (weight * mm(qp, kp, NT)).astype(BF16)
        probs[h] = p
        local[:, cols] = mm(p, v_ref[:, cols], NN)

    half, most = heads // 2, heads // 2 + heads // 4
    some_heads(inner_step, 0, half)

    gather_wait(*fwd_g)

    def scan_forward(state):
        def step(b, state):
            send_p[b] = state.astype(BF16)
            got = recv_s[b].astype(F32)
            g = got[piece : piece + 1] + got[piece + 8 : piece + 9]
            decays[pl.ds(b, 1), :] = g
            return g * state + got[:piece]

        return lax.fori_loop(0, group, step, state)

    def first_forward():
        def go():
            send_t[...] = scan_forward(jnp.zeros((piece, hd), F32)).astype(BF16)
            total_copy(*fwd_t).start()

        owner_only(place, go)
        spread_start(*fwd_s)

    def second_forward():
        def go():
            total_copy(*fwd_t).wait_recv()
            scan_forward(recv_t[...].astype(F32))

        owner_only(place, go)
        spread_start(*fwd_s)

    pl.when(jnp.logical_not(upper))(first_forward)
    some_heads(inner_step, half, most)
    pl.when(upper)(second_forward)
    some_heads(inner_step, most, heads)

    w_copy.wait()
    cot_copy.wait()
    partners(lambda k: cot_arrival(k).wait_recv(), 1, nt)
    chunk = 2 * hd if heads % 2 == 0 else hd

    def outgrad_step(c, carry):
        part = pl.ds(pl.multiple_of(c * chunk, chunk), chunk)
        outgrad[:, part] = mm(cot[...], w[part, :], NT)
        return carry

    lax.fori_loop(0, heads * hd // chunk, outgrad_step, 0)

    def head_rows(buffer, h):
        parts = [buffer[h * per_head + r] for r in range(per_head)]
        return parts[0] if per_head == 1 else jnp.concatenate(parts, axis=0)

    def norm_step(h, cols):
        qp = jnp.maximum(q_ref[:, cols], 0)
        es = escale[h]
        mixed = local[:, cols] + es * mm(qp, head_rows(prefix, h), NN)
        inv = lax.rsqrt(jnp.mean(mixed * mixed, axis=1, keepdims=True) + EPSILON)
        gain = gain_ref[:, cols]
        attended[:, cols] = (mixed * inv * gain).astype(BF16)
        gained = outgrad[:, cols] * gain
        along = jnp.mean(mixed * gained, axis=1, keepdims=True)
        mg = (inv * gained - mixed * (inv * inv * inv * along)).astype(BF16)
        mixgrad[:, cols] = mg
        sq = (es * qp.astype(F32)).astype(BF16)
        grad = mm(sq, mg, TN).astype(BF16)
        for r in range(per_head):
            send_g[h * per_head + r] = grad[r * piece : (r + 1) * piece]

    if direct:
        norm_step(place, columns(place))
        from_owner(*fwd_s, 1).wait_recv()
        norm_step(source(1), columns(source(1)))
        to_owner(*bwd_g, group - 1).start()

        def norm_pair(i, carry):
            k = 2 * i
            from_owner(*fwd_s, k).wait_recv()
            from_owner(*fwd_s, k + 1).wait_recv()
            norm_step(source(k), columns(source(k)))
            norm_step(source(k + 1), columns(source(k + 1)))
            to_owner(*bwd_g, group - k).start()
            to_owner(*bwd_g, group - k - 1).start()
            return carry

        lax.fori_loop(1, group // 2, norm_pair, 0)
        keep_mine(*bwd_g)
    else:
        spread_wait(*fwd_s)
        some_heads(norm_step, 0, heads)
        gather_start(*bwd_g)

    step_cols = 512

    def project(c, carry):
        part = pl.ds(pl.multiple_of(c * step_cols, step_cols), step_cols)
        part_o[:, part] = mm(attended[...], w[:, part], NN).astype(BF16)
        return carry

    half_cols = wide // step_cols // 2
    lax.fori_loop(0, half_cols, project, 0)

    def out_copy(k):
        d = lax.rem(my_t + k, nt)
        return pltpu.make_async_remote_copy(
            part_o.at[pl.ds(pl.multiple_of(d * rows_t, 16), rows_t)], recv_o.at[k - 1],
            o_send.at[k], o_recv.at[k], device_id={"tensor": d}, device_id_type=MESH)

    gather_wait(*bwd_g)

    def scan_backward(state):
        def step(i, state):
            b = group - 1 - i
            send_l[b] = state.astype(BF16)
            return decays[pl.ds(b, 1), :] * state + recv_g[b].astype(F32)

        return lax.fori_loop(0, group, step, state)

    def first_backward():
        def go():
            send_u[...] = scan_backward(jnp.zeros((piece, hd), F32)).astype(BF16)
            total_copy(*bwd_t).start()

        owner_only(place, go)
        spread_start(*bwd_s)

    def second_backward():
        def go():
            total_copy(*bwd_t).wait_recv()
            scan_backward(recv_u[...].astype(F32))

        owner_only(place, go)
        spread_start(*bwd_s)

    def grad_step(h, cols):
        qp = jnp.maximum(q_ref[:, cols], 0)
        kp = jnp.maximum(k_ref[:, cols], 0)
        mg = mixgrad[:, cols]
        sg = (weights[h] * mm(mg, v_ref[:, cols], NT)).astype(BF16)
        vlocal[:, cols] = mm(probs[h], mg, TN)
        klocal[:, cols] = mm(sg, qp, TN)
        qg = mm(sg, kp, NN) + escale[h] * mm(mg, head_rows(prefix, h), NT)
        qg_ref[:, cols] = jnp.where(qp.astype(F32) > 0, qg, 0.0).astype(BF16)

    early = heads // 2
    pl.when(upper)(first_backward)
    lax.fori_loop(half_cols, wide // step_cols, project, 0)
    partners(lambda k: out_copy(k).start(), 1, nt)
    some_heads(grad_step, 0, early)
    pl.when(jnp.logical_not(upper))(second_backward)
    some_heads(grad_step, early, heads)

    partners(lambda k: out_copy(k).wait_recv(), 1, nt)

    def total_out(c, carry):
        part = pl.ds(pl.multiple_of(c * step_cols, step_cols), step_cols)
        total = part_o[my_rows, part].astype(F32)
        for k in range(1, nt):
            total += recv_o[k - 1, :, part].astype(F32)
        out_ref[:, part] = total.astype(BF16)
        return carry

    lax.fori_loop(0, wide // step_cols, total_out, 0)

    def last_step(h, cols):
        lat = head_rows(later, h)
        vg_ref[:, cols] = (vlocal[:, cols] + mm(decayed[:, cols], lat, NN)).astype(BF16)
        kg = klocal[:, cols] + kscale[h] * mm(v_ref[:, cols], lat, NT)
        kg_ref[:, cols] = jnp.where(k_ref[:, cols].astype(F32) > 0, kg, 0.0).astype(BF16)

    if direct:
        last_step(place, columns(place))
        from_owner(*bwd_s, 1).wait_recv()
        last_step(source(1), columns(source(1)))

        def last_pair(i, carry):
            k = 2 * i
            from_owner(*bwd_s, k).wait_recv()
            from_owner(*bwd_s, k + 1).wait_recv()
            last_step(source(k), columns(source(k)))
            last_step(source(k + 1), columns(source(k + 1)))
            return carry

        lax.fori_loop(1, group // 2, last_pair, 0)
    else:
        spread_wait(*bwd_s)
        some_heads(last_step, 0, heads)

    partners(lambda k: cot_remote(k).wait_send(), 1, nt)
    partners(lambda k: out_copy(k).wait_send(), 1, nt)
    sends_wait(fwd_g, fwd_s)
    sends_wait(bwd_g, bwd_s)
    pl.when(jnp.logical_not(upper))(
        lambda: owner_only(place, lambda: total_copy(*fwd_t).wait_send()))
    pl.when(upper)(lambda: owner_only(place, lambda: total_copy(*bwd_t).wait_send()))


def write_kernel(*refs):
    count = (len(refs) - 1) // 2
    sems = refs[-1]
    copies = [
        pltpu.make_async_copy(refs[i], refs[count + i], sems.at[i]) for i in range(count)
    ]
    for copy in copies:
        copy.start()
    for copy in copies:
        copy.wait()


def on_device(n, nt, q, k, v, ld, sid, gain, w, cot):
    tok, width = q.shape
    heads = ld.shape[0]
    hd = width // heads
    wide = w.shape[1]
    rows_t = cot.shape[0]
    group = n // 2
    owners = owners_of(width, hd, group)
    piece = width // owners
    vmem = pl.BlockSpec(memory_space=pltpu.VMEM)
    hbm = pl.BlockSpec(memory_space=pl.ANY)
    dma = pltpu.SemaphoreType.DMA
    flat16 = pltpu.VMEM((tok, width), BF16)
    flat32 = pltpu.VMEM((tok, width), F32)
    wide_h = pltpu.VMEM((heads, tok, hd), F32)
    one = pltpu.VMEM((piece, hd), BF16)
    by_owner = pltpu.VMEM((owners, piece, hd), BF16)
    by_place = pltpu.VMEM((group, piece, hd), BF16)
    shapes = ((rows_t, wide), (tok, width), (tok, width), (tok, width))
    cost = pl.CostEstimate(
        flops=4 * tok * width * wide + 14 * tok * tok * width + 12 * tok * width * hd,
        bytes_accessed=2 * width * wide + 16 * tok * width,
        transcendentals=heads * tok * tok,
    )
    args = [
        pltpu.with_memory_space_constraint(x, pltpu.HBM)
        for x in (ld, sid, gain.reshape(1, -1), q, k, v, w, cot)
    ]
    results = pl.pallas_call(
        functools.partial(kernel, n, nt, owners),
        out_shape=tuple(pltpu.VMEM(shape, BF16) for shape in shapes),
        in_specs=[pl.BlockSpec(memory_space=pltpu.HBM)] * 8,
        out_specs=(vmem,) * 4,
        scratch_shapes=[
            pltpu.VMEM(ld.shape, F32),
            pltpu.VMEM(sid.shape, jnp.int32),
            pltpu.VMEM((1, width), F32),
            flat16, flat16, flat16,
            pltpu.VMEM(w.shape, BF16),
            pltpu.VMEM((tok, wide), BF16),
            pltpu.VMEM((tok, tok), F32),
            pltpu.VMEM((heads, tok), F32),
            wide_h, wide_h, wide_h,
            flat16,
            pltpu.VMEM((heads, tok, tok), F32),
            pltpu.VMEM((heads, tok, tok), BF16),
            flat32, flat32, flat16, flat16, flat32, flat32,
            pltpu.VMEM((group, hd), F32),
            pltpu.VMEM((owners, piece + 16, hd), BF16),
            pltpu.VMEM((group, piece + 16, hd), BF16),
            by_place, by_owner, by_owner, by_place, by_place, by_owner,
            one, one, one, one,
            pltpu.VMEM((tok, wide), BF16),
            pltpu.VMEM((max(nt - 1, 1), rows_t, wide), BF16),
            dma((3,)), dma, dma, dma, dma, dma, dma((nt,)), dma((nt,)),
            dma((group,)), dma((group,)), dma((group,)), dma((group,)),
            dma((group,)), dma((group,)), dma((group,)), dma((group,)),
            dma((nt,)), dma((nt,)), dma, dma, dma, dma,
        ],
        compiler_params=pltpu.CompilerParams(
            collective_id=0, has_side_effects=True, vmem_limit_bytes=50 * 1024 * 1024
        ),
        cost_estimate=cost,
    )(*args)
    return pl.pallas_call(
        write_kernel,
        out_shape=tuple(jax.ShapeDtypeStruct(shape, BF16) for shape in shapes),
        in_specs=[hbm] * 4,
        out_specs=(hbm,) * 4,
        scratch_shapes=[dma((4,))],
        compiler_params=pltpu.CompilerParams(vmem_limit_bytes=2 * 1024 * 1024),
    )(*results)


def solution(mesh):
    n, nt = mesh.shape["tm"], mesh.shape["tensor"]
    return jax.shard_map(
        functools.partial(on_device, n, nt),
        mesh=mesh,
        in_specs=(
            P("tm", "tensor"),
            P("tm", "tensor"),
            P("tm", "tensor"),
            P("tensor", "tm"),
            P("tm"),
            P("tensor"),
            P("tensor", None),
            P(("tm", "tensor"), None),
        ),
        out_specs=(
            P(("tm", "tensor"), None),
            P("tm", "tensor"),
            P("tm", "tensor"),
            P("tm", "tensor"),
        ),
        check_vma=False,
    )
```
